32 devices in a mesh: row: 8 (over z, x), col: 4 (over y, core).
Axes of the slice: x: 2, y: 2, z: 4, core: 2. Of those that a mesh axis runs over, the one named last changes fastest.
Arguments:
- factor: float32 [2, 2048, 2, 1024], P(None, 'row', None, 'col'), may hold values from -5 to 5, as said below
- update: float32 [2, 2048, 512], P(None, 'row', 'col'), may hold values from -1.5 to 1.5
Outputs:
- updated_factor: float32 [2, 2048, 2, 1024], P(None, 'row', None, 'col')
The draws below stay inside these ranges and needn't reach their ends.
Inputs may be any that keep to these rules, and one draw needn't show every extreme that they name: `factor`: in the first 2048 rows, entries to the right of the diagonal are zero and diagonal entries are positive.
All inputs are finite; a program needn't handle non-finite values.
Results may differ from the reference program's by a relative error of at most 0.0003.
Values sent between devices are 32-bit elements; how exact they have to be, the bound alone decides.
A program may use at most 128 MiB of HBM per device.

```python
import jax
import jax.numpy as jnp
from jax import lax

PANEL = 1024
PANELS = 2
K = 512
RT = 2
SPAN = 2048


def draw_factor(key, part):
    key_base, key_diag = jax.random.split(key, 2)
    shape = (RT, SPAN, PANELS, PANEL)
    global_row = jnp.arange(RT, dtype=jnp.int32)[:, None, None, None] * SPAN + jnp.arange(SPAN, dtype=jnp.int32)[None, :, None, None]
    global_col = jnp.arange(PANELS, dtype=jnp.int32)[None, None, :, None] * PANEL + jnp.arange(PANEL, dtype=jnp.int32)[None, None, None, :]
    diag_span = PANELS * PANEL
    base = jnp.clip(jax.random.normal(key_base, shape, jnp.float32), -5.0, 5.0)
    diagonal = jax.random.uniform(key_diag, shape, jnp.float32, 2.0, 4.0)
    lower_part = base * jnp.float32(diag_span) ** (-0.5)
    inside_value = jnp.where(global_col < global_row, lower_part, jnp.where(global_col == global_row, diagonal, jnp.zeros_like(base)))
    return jnp.where(global_row < diag_span, inside_value, base)


def levels(stream_key, dims, pieces, smallest, high):
    level, own = 1.0, jax.random.fold_in(stream_key, 6)
    for axis_at, blocks in pieces:
        steps = jnp.exp(jax.random.uniform(jax.random.fold_in(own, axis_at), (blocks,), jnp.float32, smallest / len(pieces), high / len(pieces)))
        level = level * jnp.repeat(steps, dims[axis_at] // blocks).reshape([-1 if axis == axis_at else 1 for axis in range(len(dims))])
    return level


def scatter_about(key, extent, width, limit, pieces=(), kind=jnp.bfloat16):
    values = width * jax.random.normal(key, extent, jnp.float32)
    if pieces:
        values = values * levels(key, extent, pieces, -0.22, 0.18)
    return jnp.clip(values, -limit, limit).astype(kind)


def setup_inputs(seed: int = 0) -> dict:
    seeds = jax.random.split(jax.random.key(seed), 3)
    return {
        "factor": draw_factor(jax.random.fold_in(seeds[2], 71), 0),
        "update": scatter_about(seeds[1], (RT, SPAN, K), 0.25, 1.5, ((1, 8), (2, 4)), jnp.float32),
    }


def reference(factor, update):
    blocks, cycle_rows, panels, panel_cols = factor.shape
    total_rows = blocks * cycle_rows
    factor_width = panels * panel_cols
    joined = jnp.concatenate([factor.reshape(total_rows, factor_width), update.reshape(total_rows, update.shape[2])], axis=1)
    outputs = []
    for panel_idx in range(panels):
        row_start = panel_idx * panel_cols
        row_end = row_start + panel_cols
        chosen = jnp.concatenate([joined[:, :row_end], joined[:, factor_width:]], axis=1)
        panel_rows = chosen[row_start:row_end]
        earlier = [prev_out[row_start:row_end] for prev_out in outputs]
        lhs_block = jnp.concatenate([panel_rows] + earlier, axis=1)
        rhs_block = jnp.concatenate([panel_rows] + [-entry for entry in earlier], axis=1)
        gram_block = jnp.dot(lhs_block.astype(jnp.float32), rhs_block.T.astype(jnp.float32), precision=lax.Precision.HIGHEST, preferred_element_type=jnp.float32)
        factor_block = jnp.linalg.cholesky(gram_block)
        solved = lax.linalg.triangular_solve(factor_block, rhs_block, left_side=True, lower=True)
        left_rows = jnp.concatenate([chosen] + outputs, axis=1)
        outputs.append(jnp.dot(left_rows.astype(jnp.float32), solved.T.astype(jnp.float32), precision=lax.Precision.HIGHEST, preferred_element_type=jnp.float32))
    stacked = jnp.stack(outputs, axis=1)
    global_row = jnp.arange(total_rows, dtype=jnp.int32)
    global_col = jnp.arange(panels, dtype=jnp.int32)[:, None] * panel_cols + jnp.arange(panel_cols, dtype=jnp.int32)[None, :]
    inside = global_col[None, :, :] <= global_row[:, None, None]
    result = jnp.where(inside, stacked, jnp.zeros_like(stacked))
    return result.reshape(blocks, cycle_rows, panels, panel_cols)
```

```python
import functools

import jax
import jax.numpy as jnp
from jax import lax
from jax.experimental import pallas as pl
from jax.experimental.pallas import tpu as pltpu
from jax.sharding import PartitionSpec as P

PANEL = 1024
PANELS = 2
B=256; H=128; GRP=8; AHEAD=3
NN=(((1,),(0,)),((),()))
NT=(((1,),(1,)),((),())); TN=(((0,),(0,)),((),()))
def split(x):
    hi=x.astype(jnp.bfloat16); return hi,(x-hi.astype(jnp.float32)).astype(jnp.bfloat16)
def dot3(a,b,dims=NT):
    (ah,al),(bh,bl)=a,b
    d=functools.partial(lax.dot_general,dimension_numbers=dims,preferred_element_type=jnp.float32)
    return d(ah,bh)+(d(ah,bl)+d(al,bh))
def small(a,b,dims=NT):
    return dot3(split(a),split(b),dims)
def wide(x):
    return jnp.broadcast_to(x, (GRP, H))


def factor_half(s_ref, a):
    rows = lax.broadcasted_iota(jnp.int32, (H, H), 0)
    cols = lax.broadcasted_iota(jnp.int32, (H, H), 1)
    s_ref[:, :H] = a
    s_ref[:, H:] = (rows == cols).astype(jnp.float32)
    sub = lax.broadcasted_iota(jnp.int32, (GRP, 1), 0)
    n = H // GRP
    live = {}
    ahead = None
    for g in range(n):
        j = g * GRP
        near = range(g, min(g + AHEAD + 1, n))
        for h in near:
            if h not in live:
                live[h] = [s_ref[h * GRP : (h + 1) * GRP, :H], s_ref[h * GRP : (h + 1) * GRP, H:]]
        cb = {h: [wide(live[h][0][:, j + b : j + b + 1]) for b in range(GRP)] for h in near if h > g or ahead is None}
        if ahead is not None:
            cb[g] = ahead
        ahead = None
        if g + 1 < n:
            ahead = [wide(live[g + 1][0][:, j + GRP + b : j + GRP + b + 1]) for b in range(GRP)]
        scale = None
        for i in range(GRP):
            piv = [wide(cb[g][b][i : i + 1, :]) for b in range(i, GRP)]
            rs = lax.rsqrt(piv[0])
            inv = rs * rs
            scale = rs if scale is None else jnp.where(sub == i, rs, scale)
            u = [wide(x[i : i + 1, :]) for x in live[g]]
            for h in near:
                p = cb[h][i]
                if h == g:
                    p = jnp.where(sub > i, p, 0.0)
                m = p * inv
                live[h] = [x - m * y for x, y in zip(live[h], u)]
                for b in range(i + 1, GRP):
                    cb[h][b] = cb[h][b] - (p * piv[b - i]) * inv
                if h == g + 1:
                    ahead = [x - m * wide(p[b : b + 1, :]) for b, x in enumerate(ahead)]
        done = [x * scale for x in live.pop(g)]
        s_ref[j : j + GRP, :H], s_ref[j : j + GRP, H:] = done
        lo = (g + AHEAD + 1) * GRP
        if lo < H:
            r = jnp.concatenate(done, axis=1)
            s_ref[lo:, :] = s_ref[lo:, :] - small(r[:, lo:H], r, TN)
    u = jnp.where(rows <= cols, s_ref[:, :H], 0.0)
    return u, s_ref[:, H:]


def factor_panel(nrow, ncol, g, ph, plo, inv, s_ref):
    def step(k, _):
        kc = pl.ds(pl.multiple_of(k * B, B), B)
        a = g[k, :, kc]
        u1, v1 = factor_half(s_ref, a[:H, :H])
        l21 = small(a[H:, :H], v1, NT)
        u2, v2 = factor_half(s_ref, a[H:, H:] - small(l21, l21, NT))
        zero = jnp.zeros((H, H), jnp.float32)
        inv[:H, :H] = v1
        inv[:H, H:] = zero
        inv[H:, :H] = -small(v2, small(l21, v1, NN), NN)
        inv[H:, H:] = v2
        g[k, :H, kc] = jnp.concatenate([u1.T, zero], axis=1)
        g[k, H:, kc] = jnp.concatenate([l21, u2.T], axis=1)
        iv = split(inv[...])

        def panel(i, _):
            p = dot3(split(g[i, :, kc]), iv)
            g[i, :, kc] = p
            ph[i], plo[i] = split(p)
            return 0

        lax.fori_loop(k + 1, nrow, panel, 0)

        def colup(j, _):
            jc = pl.ds(pl.multiple_of(j * B, B), B)
            w = (ph[j], plo[j])

            def rowup(i, _):
                g[i, :, jc] = g[i, :, jc] - dot3((ph[i], plo[i]), w)
                return 0

            lax.fori_loop(j, nrow, rowup, 0)
            return 0

        lax.fori_loop(k + 1, ncol, colup, 0)
        return 0

    lax.fori_loop(0, ncol, step, 0)


def panel_kernel(p, ntile, nown, sizes, *refs):
    tc, uc, ncol_dev = sizes
    per = PANEL // B
    first = p * per
    nrow = ntile - first + nown
    if p == 0:
        idx, d_ref, o_ref, out_ref, f_out, xh, xl, g, ph, plo, inv, s_ref = refs
    else:
        idx, d_ref, o_ref, d1_ref, o1_ref, f_in, out_ref, xh, xl, g, ph, plo, inv, s_ref = refs
    width = PANEL + uc * ncol_dev
    for i in range(nrow):
        t = i + first
        src = d_ref if t < ntile else o_ref
        at = (i if p else t) if t < ntile else t - ntile
        for c in range(ncol_dev):
            xh[i, :, c * tc : (c + 1) * tc], xl[i, :, c * tc : (c + 1) * tc] = split(src[at, c, :, :tc])
            lo = PANEL + c * uc
            xh[i, :, lo : lo + uc], xl[i, :, lo : lo + uc] = split(src[at, c, :, tc:])
        if p:
            src = d1_ref if t < ntile else o1_ref
            for c in range(ncol_dev):
                lo = width + c * tc
                xh[i, :, lo : lo + tc], xl[i, :, lo : lo + tc] = split(src[at, c])
            xh[i, :, width + PANEL :], xl[i, :, width + PANEL :] = split(f_in[i])
    full = width + p * PANEL

    def gram_col(j, _):
        jc = pl.ds(pl.multiple_of(j * B, B), B)

        def gram_row(i, _):
            v = dot3((xh[i, :, :full], xl[i, :, :full]), (xh[j, :, :full], xl[j, :, :full]))
            if p:
                v = v - dot3((xh[i, :, full:], xl[i, :, full:]), (xh[j, :, full:], xl[j, :, full:]))
            g[i, :, jc] = v
            return 0

        lax.fori_loop(j, nrow, gram_row, 0)
        return 0

    lax.fori_loop(0, per, gram_col, 0)
    factor_panel(nrow, per, g, ph, plo, inv, s_ref)
    if p == 0:
        f_out[...] = g[per:]
    oc = pl.ds(pl.multiple_of(idx[1] * tc, tc), tc)
    if nown == 1:
        r = idx[0] - first
        t = g[jnp.maximum(r, 0), :, oc]
        keep = idx[1] * (tc // B) <= r
        out_ref[0] = jnp.where(keep, t, 0.0)
        out_ref[1] = g[nrow - 1, :, oc]
    else:
        for e in range(2):
            out_ref[e] = g[nrow - 2 + e, :, oc]


def run_panel(p, idx, ntile, nown, sizes, *arrays):
    tc, uc, nc = sizes
    per = PANEL // B
    nrow = ntile - p * per + nown
    width = PANEL + uc * nc + p * 2 * PANEL
    vm = pl.BlockSpec(memory_space=pltpu.VMEM)
    shape = [jax.ShapeDtypeStruct((2, B, tc), jnp.float32)]
    if p == 0:
        shape.append(jax.ShapeDtypeStruct((nrow - per, B, PANEL), jnp.float32))
    return pl.pallas_call(
        functools.partial(panel_kernel, p, ntile, nown, sizes),
        out_shape=shape,
        in_specs=[pl.BlockSpec(memory_space=pltpu.SMEM)] + [vm] * len(arrays),
        out_specs=[vm] * len(shape),
        scratch_shapes=[
            pltpu.VMEM((nrow, B, width), jnp.bfloat16),
            pltpu.VMEM((nrow, B, width), jnp.bfloat16),
            pltpu.VMEM((nrow, B, PANEL), jnp.float32),
            pltpu.VMEM((nrow, B, B), jnp.bfloat16),
            pltpu.VMEM((nrow, B, B), jnp.bfloat16),
            pltpu.VMEM((B, B), jnp.float32),
            pltpu.VMEM((H, 2 * H), jnp.float32),
        ],
        cost_estimate=pl.CostEstimate(flops=60_000_000_000, bytes_accessed=30_000_000, transcendentals=0),
        compiler_params=pltpu.CompilerParams(vmem_limit_bytes=60 * 2**20),
        name="panel%d" % p,
    )(idx, *arrays)


def per_device(factor, update):
    blocks, tile_rows, panels, tc = factor.shape
    uc = update.shape[2]
    nr, nc = lax.axis_size("row"), lax.axis_size("col")
    r, c = lax.axis_index("row"), lax.axis_index("col")
    ntile = PANELS * PANEL // tile_rows
    whole_rows = nr == ntile
    nown = blocks - 1 if whole_rows else blocks
    sizes = (tc, uc, nc)
    xa = jnp.concatenate([factor[:, :, 0], update], axis=2)
    xb = factor[:, :, 1]

    def diag(x):
        if whole_rows:
            return lax.all_gather(x, ("row", "col")).reshape(ntile, nc, *x.shape)
        tiles = [lax.psum(jnp.where(r == t, x, 0.0), "row") for t in range(ntile)]
        return jnp.moveaxis(lax.all_gather(jnp.stack(tiles), "col"), 0, 1)

    def own(x):
        return jnp.moveaxis(lax.all_gather(x[blocks - nown :], "col"), 0, 1)

    da, oa = diag(xa[0]), own(xa)
    xb = xb + (da[0, 0, 0, 0] + oa[0, 0, 0, 0]) * 0.0
    db, ob = diag(xb[0]), own(xb)
    idx = jnp.stack([r, c]).astype(jnp.int32)
    out0, f0 = run_panel(0, idx, ntile, nown, sizes, da, oa)
    (out1,) = run_panel(1, idx, ntile, nown, sizes, da[ntile // 2 :], oa, db[ntile // 2 :], ob, f0)
    out = jnp.stack([out0, out1], axis=2)
    if not whole_rows:
        rows = (
            jnp.arange(blocks)[:, None] * (nr * tile_rows) + r * tile_rows + jnp.arange(tile_rows)
        )
        cols = jnp.arange(panels)[:, None] * PANEL + c * tc + jnp.arange(tc)
        out = jnp.where(cols <= rows[:, :, None, None], out, 0.0)
    return out


def solution(mesh):
    in_specs = (P(None, "row", None, "col"), P(None, "row", "col"))
    out_specs = P(None, "row", None, "col")
    return jax.shard_map(
        per_device, mesh=mesh, in_specs=in_specs, out_specs=out_specs, check_vma=False
    )
```

```python
import functools

import jax
import jax.numpy as jnp
from jax import lax
from jax.experimental import pallas as pl
from jax.experimental.pallas import tpu as pltpu
from jax.sharding import PartitionSpec as P

PANEL = 1024
PANELS = 2
B=256; H=128; GRP=8; AHEAD=3
NN=(((1,),(0,)),((),()))
NT=(((1,),(1,)),((),())); TN=(((0,),(0,)),((),()))
def split(x):
    hi=x.astype(jnp.bfloat16); return hi,(x-hi.astype(jnp.float32)).astype(jnp.bfloat16)
def dot3(a,b,dims=NT):
    (ah,al),(bh,bl)=a,b
    d=functools.partial(lax.dot_general,dimension_numbers=dims,preferred_element_type=jnp.float32)
    return d(ah,bh)+(d(ah,bl)+d(al,bh))
def small(a,b,dims=NT):
    return dot3(split(a),split(b),dims)
def wide(x):
    return jnp.broadcast_to(x, (GRP, H))


def factor_half(s_ref, a, hook=None):
    rows = lax.broadcasted_iota(jnp.int32, (H, H), 0)
    cols = lax.broadcasted_iota(jnp.int32, (H, H), 1)
    s_ref[:, :H] = a
    s_ref[:, H:] = (rows == cols).astype(jnp.float32)
    sub = lax.broadcasted_iota(jnp.int32, (GRP, 1), 0)
    n = H // GRP
    live = {}
    ahead = None
    for g in range(n):
        j = g * GRP
        near = range(g, min(g + AHEAD + 1, n))
        for h in near:
            if h not in live:
                live[h] = [s_ref[h * GRP : (h + 1) * GRP, :H], s_ref[h * GRP : (h + 1) * GRP, H:]]
        cb = {h: [wide(live[h][0][:, j + b : j + b + 1]) for b in range(GRP)] for h in near if h > g or ahead is None}
        if ahead is not None:
            cb[g] = ahead
        ahead = None
        if g + 1 < n:
            ahead = [wide(live[g + 1][0][:, j + GRP + b : j + GRP + b + 1]) for b in range(GRP)]
        scale = None
        for i in range(GRP):
            if hook is not None:
                hook(g, i)
            piv = [wide(cb[g][b][i : i + 1, :]) for b in range(i, GRP)]
            rs = lax.rsqrt(piv[0])
            inv = rs * rs
            scale = rs if scale is None else jnp.where(sub == i, rs, scale)
            u = [wide(x[i : i + 1, :]) for x in live[g]]
            for h in near:
                p = cb[h][i]
                if h == g:
                    p = jnp.where(sub > i, p, 0.0)
                m = p * inv
                live[h] = [x - m * y for x, y in zip(live[h], u)]
                for b in range(i + 1, GRP):
                    cb[h][b] = cb[h][b] - (p * piv[b - i]) * inv
                if h == g + 1:
                    ahead = [x - m * wide(p[b : b + 1, :]) for b, x in enumerate(ahead)]
        done = [x * scale for x in live.pop(g)]
        s_ref[j : j + GRP, :H], s_ref[j : j + GRP, H:] = done
        lo = (g + AHEAD + 1) * GRP
        if lo < H:
            r = jnp.concatenate(done, axis=1)
            s_ref[lo:, :] = s_ref[lo:, :] - small(r[:, lo:H], r, TN)
    u = jnp.where(rows <= cols, s_ref[:, :H], 0.0)
    return u, s_ref[:, H:]


def factor_panel(nrow, ncol, g, ph, plo, inv, s_ref):
    def step(k, _):
        kc = pl.ds(pl.multiple_of(k * B, B), B)
        a = g[k, :, kc]
        u1, v1 = factor_half(s_ref, a[:H, :H])
        l21 = small(a[H:, :H], v1, NT)
        u2, v2 = factor_half(s_ref, a[H:, H:] - small(l21, l21, NT))
        zero = jnp.zeros((H, H), jnp.float32)
        inv[:H, :H] = v1
        inv[:H, H:] = zero
        inv[H:, :H] = -small(v2, small(l21, v1, NN), NN)
        inv[H:, H:] = v2
        g[k, :H, kc] = jnp.concatenate([u1.T, zero], axis=1)
        g[k, H:, kc] = jnp.concatenate([l21, u2.T], axis=1)
        iv = split(inv[...])

        def panel(i, _):
            p = dot3(split(g[i, :, kc]), iv)
            g[i, :, kc] = p
            ph[i], plo[i] = split(p)
            return 0

        lax.fori_loop(k + 1, nrow, panel, 0)

        def colup(j, _):
            jc = pl.ds(pl.multiple_of(j * B, B), B)
            w = (ph[j], plo[j])

            def rowup(i, _):
                g[i, :, jc] = g[i, :, jc] - dot3((ph[i], plo[i]), w)
                return 0

            lax.fori_loop(j, nrow, rowup, 0)
            return 0

        lax.fori_loop(k + 1, ncol, colup, 0)
        return 0

    lax.fori_loop(0, ncol, step, 0)


def panel_kernel(p, ntile, nown, sizes, *refs):
    tc, uc, ncol_dev = sizes
    per = PANEL // B
    first = p * per
    nrow = ntile - first + nown
    if p == 0:
        idx, d_ref, o_ref, out_ref, f_out, xh, xl, g, ph, plo, inv, s_ref = refs
    else:
        idx, d_ref, o_ref, d1_ref, o1_ref, f_in, out_ref, xh, xl, g, ph, plo, inv, s_ref = refs
    width = PANEL + uc * ncol_dev
    for i in range(nrow):
        t = i + first
        src = d_ref if t < ntile else o_ref
        at = (i if p else t) if t < ntile else t - ntile
        for c in range(ncol_dev):
            xh[i, :, c * tc : (c + 1) * tc], xl[i, :, c * tc : (c + 1) * tc] = split(src[at, c, :, :tc])
            lo = PANEL + c * uc
            xh[i, :, lo : lo + uc], xl[i, :, lo : lo + uc] = split(src[at, c, :, tc:])
        if p:
            src = d1_ref if t < ntile else o1_ref
            for c in range(ncol_dev):
                lo = width + c * tc
                xh[i, :, lo : lo + tc], xl[i, :, lo : lo + tc] = split(src[at, c])
            xh[i, :, width + PANEL :], xl[i, :, width + PANEL :] = split(f_in[i])
    full = width + p * PANEL

    def gram_col(j, _):
        jc = pl.ds(pl.multiple_of(j * B, B), B)

        def gram_row(i, _):
            v = dot3((xh[i, :, :full], xl[i, :, :full]), (xh[j, :, :full], xl[j, :, :full]))
            if p:
                v = v - dot3((xh[i, :, full:], xl[i, :, full:]), (xh[j, :, full:], xl[j, :, full:]))
            g[i, :, jc] = v
            return 0

        lax.fori_loop(j, nrow, gram_row, 0)
        return 0

    lax.fori_loop(0, per, gram_col, 0)
    factor_panel(nrow, per, g, ph, plo, inv, s_ref)
    if p == 0:
        f_out[...] = g[per:]
    oc = pl.ds(pl.multiple_of(idx[1] * tc, tc), tc)
    if nown == 1:
        r = idx[0] - first
        t = g[jnp.maximum(r, 0), :, oc]
        keep = idx[1] * (tc // B) <= r
        out_ref[0] = jnp.where(keep, t, 0.0)
        out_ref[1] = g[nrow - 1, :, oc]
    else:
        for e in range(2):
            out_ref[e] = g[nrow - 2 + e, :, oc]


TASKS = 3
NTOP = 8


def tri(i, m):
    return i * (i + 1) // 2 + m


def xtile(i, m):
    return 2 * (NTOP + 1) + tri(i, m)


def ltile(i, m):
    return 2 * (NTOP + 1) + tri(NTOP, NTOP) + i * (i - 1) // 2 + m


NW = tri(NTOP, NTOP) + 1
NPOOL = ltile(NTOP, NTOP)


def plan(slots, late=()):
    jobs = []
    for i in range(NTOP + 1):
        for m in range(min(i, NTOP - 1) + 1):
            due = m if m < i else m - 1
            for q in range(2):
                jobs.append((due, 0, (tri(i, m), 2 * i + q, 2 * m + q, 1)))
            for q in range(m + 1):
                jobs.append((due, 0, (tri(i, m), xtile(i, q), xtile(m, q), 1)))
            for q in range(m if m < i else m - 1):
                jobs.append((due, q + 1, (tri(i, m), ltile(i, q), ltile(m, q), -1)))
    first = [t for due, _, t in jobs if due < 0]
    jobs = sorted((j for j in jobs if j[0] >= 0), key=lambda j: (j[0], -j[1]))
    table = []
    for k in range(NTOP):
        now = [j for j in jobs if j[1] <= k][:slots]
        jobs = [j for j in jobs if j not in now]
        assert not jobs or jobs[0][0] > k
        table += [t for _, _, t in now] + [(NW - 1, 0, 0, 1)] * (slots - len(now))
    return first, table


def split_into(ph, plo, t, x, lanes=slice(None)):
    ph[t, :, lanes], plo[t, :, lanes] = split(x)


def top_kernel(slots, first, pos, tab, g_ref, o_ref, out_ref, ph, plo, w, inv, s_ref, stage, sems):
    n = NTOP
    rows = [g_ref.at[i] for i in range(n)] + [o_ref]

    def fetch(i):
        return pltpu.make_async_copy(rows[i], stage.at[i % 2], sems.at[i % 2])

    fetch(0).start()
    for i in range(n + 1):
        if i < n:
            fetch(i + 1).start()
        fetch(i).wait()
        for c in range(4):
            lo = (c % 2) * H
            split_into(ph, plo, 2 * i + c // 2, stage[i % 2, c, 0], slice(lo, lo + H))
            for p in range(2):
                m = 4 * p + c
                if m <= i:
                    for h in range(2):
                        split_into(ph, plo, xtile(i, m), stage[i % 2, c, 1 + 2 * p + h], slice(h * H, (h + 1) * H))

    def clear(t, _):
        w[t] = jnp.zeros((B, B), jnp.float32)
        return 0

    lax.fori_loop(0, NW, clear, 0)

    def product(a, b):
        return dot3((ph[a], plo[a]), (ph[b], plo[b]))

    for t, a, b, s in first:
        w[t] = w[t] + s * product(a, b)

    def step(k, _):
        def task(half, g, i):
            for u in range(TASKS):
                if (g % 2) * 8 + i == u * 16 // TASKS:
                    at = k * slots + half * (slots // 2) + (g // 2) * TASKS + u
                    t = tab[at, 0]
                    sign = tab[at, 3].astype(jnp.float32)
                    w[t] = w[t] + sign * product(tab[at, 1], tab[at, 2])

        d = tri(k, k)
        u1, v1 = factor_half(s_ref, w[d, :H, :H], functools.partial(task, 0))
        l21 = small(w[d, H:, :H], v1, NT)
        u2, v2 = factor_half(s_ref, w[d, H:, H:] - small(l21, l21, NT), functools.partial(task, 1))
        zero = jnp.zeros((H, H), jnp.float32)
        inv[:H, :H] = v1
        inv[:H, H:] = zero
        inv[H:, :H] = -small(v2, small(l21, v1, NN), NN)
        inv[H:, H:] = v2
        w[d, :H, :] = jnp.concatenate([u1.T, zero], axis=1)
        w[d, H:, :] = jnp.concatenate([l21, u2.T], axis=1)
        iv = split(inv[...])

        def solve(i, _):
            t = tri(i, k)
            x = dot3(split(w[t]), iv)
            w[t] = x
            split_into(ph, plo, ltile(i, k), x)
            return 0

        lax.fori_loop(k + 1, n + 1, solve, 0)
        t = tri(k + 1, k + 1)
        a = ltile(k + 1, k)
        w[t] = w[t] - product(a, a)
        return 0

    lax.fori_loop(0, n, step, 0)
    r = pos[0]
    for p in range(2):
        m = pos[1] + 4 * p
        out_ref[0, p] = jnp.where(m <= r, w[jnp.where(m <= r, tri(r, m), 0)], 0.0)
        out_ref[1, p] = w[tri(n, m)]


def run_top(pos, gathered, own):
    slots = 2 * (H // GRP) * TASKS // 2
    first, table = plan(slots)
    any_ = pl.BlockSpec(memory_space=pl.ANY)
    smem = pl.BlockSpec(memory_space=pltpu.SMEM)
    return pl.pallas_call(
        functools.partial(top_kernel, slots, first),
        out_shape=jax.ShapeDtypeStruct((2, 2, B, B), jnp.float32),
        in_specs=[smem, smem, any_, any_],
        out_specs=pl.BlockSpec(memory_space=pltpu.VMEM),
        scratch_shapes=[
            pltpu.VMEM((NPOOL, B, B), jnp.bfloat16),
            pltpu.VMEM((NPOOL, B, B), jnp.bfloat16),
            pltpu.VMEM((NW, B, B), jnp.float32),
            pltpu.VMEM((B, B), jnp.float32),
            pltpu.VMEM((H, 2 * H), jnp.float32),
            pltpu.VMEM((2, 4, 5, B, H), jnp.float32),
            pltpu.SemaphoreType.DMA((2,)),
        ],
        cost_estimate=pl.CostEstimate(flops=40_000_000_000, bytes_accessed=25_000_000, transcendentals=0),
        compiler_params=pltpu.CompilerParams(vmem_limit_bytes=58 * 2**20),
        name="top",
    )(pos, jnp.asarray(table, jnp.int32), gathered, own)


def gather_kernel(x_ref, g_ref, o_ref, zs, zr, xs, xr, ys, yr, cs, cr, ls):
    r, c = lax.axis_index("row"), lax.axis_index("col")
    rx = r + 1 - 2 * (r % 2)
    cy = (c + 2) % 4
    ck = c + 1 - 2 * (c % 2)
    nr = 8
    line = [((r + 2 * d) % nr, c) for d in range(1, 4)]
    x_dev, y_dev, k_dev = (rx, c), (r, cy), (r, ck)

    barrier = pltpu.get_barrier_semaphore()
    for dev in line + [x_dev, y_dev, k_dev]:
        pl.semaphore_signal(barrier, inc=1, device_id=dev, device_id_type=pl.DeviceIdType.MESH)
    pl.semaphore_wait(barrier, 6)

    def copy(src, dst, dev, ssem, rsem):
        return pltpu.make_async_remote_copy(
            src_ref=src, dst_ref=dst, send_sem=ssem, recv_sem=rsem, device_id=dev, device_id_type=pl.DeviceIdType.MESH
        )

    def each(piece, act):
        i, j = piece
        for n, cond in ((1, i < j), (3, (i >= j) & (i < 4 + j)), (5, i >= 4 + j)):
            pl.when(cond)(functools.partial(act, n))

    sent = []

    def send(piece, dev, ssem, rsem, mine=False):
        i, j = piece

        def make(n):
            src = x_ref.at[0, pl.ds(0, n)] if mine else g_ref.at[i, j, pl.ds(0, n)]
            return copy(src, g_ref.at[i, j, pl.ds(0, n)], dev, ssem, rsem)

        each(piece, lambda n: make(n).start())
        sent.append((piece, lambda n: make(n).wait_send()))

    def arrived(piece, rsem):
        i, j = piece
        at = lambda n: g_ref.at[i, j, pl.ds(0, n)]
        each(piece, lambda n: copy(at(n), at(n), k_dev, cs.at[0], rsem).wait_recv())

    keep = [
        pltpu.make_async_copy(x_ref.at[0], g_ref.at[r, c], ls.at[0]),
        pltpu.make_async_copy(x_ref.at[1], o_ref.at[c], ls.at[1]),
    ]
    for d in range(3):
        send((r, c), line[d], zs.at[d], zr.at[d], True)
    send((r, c), x_dev, xs.at[0], xr.at[0], True)
    send((r, c), y_dev, ys.at[0], yr.at[0], True)
    send((r, c), k_dev, cs.at[0], cr.at[0], True)
    for cp in keep:
        cp.start()
    low = [
        copy(x_ref.at[1], o_ref.at[c], y_dev, ys.at[6], yr.at[6]),
        copy(x_ref.at[1], o_ref.at[c], k_dev, cs.at[16], cr.at[16]),
        copy(o_ref.at[cy], o_ref.at[cy], k_dev, cs.at[17], cr.at[17]),
    ]
    low[0].start()
    low[1].start()
    for d in range(1, 4):
        p = ((r + nr - 2 * d) % nr, c)
        arrived(p, zr.at[d - 1])
        send(p, x_dev, xs.at[d], xr.at[d])
        send(p, y_dev, ys.at[d], yr.at[d])
        send(p, k_dev, cs.at[d], cr.at[d])
    for s in range(4):
        px = ((rx + nr - 2 * s) % nr, c)
        arrived(px, xr.at[s])
        if s % 2:
            send(px, y_dev, ys.at[4 + s // 2], yr.at[4 + s // 2])
        send(px, k_dev, cs.at[4 + s], cr.at[4 + s])
        py = ((r + nr - 2 * s) % nr, cy)
        arrived(py, yr.at[s])
        if s % 2 == 0:
            send(py, x_dev, xs.at[4 + s // 2], xr.at[4 + s // 2])
        send(py, k_dev, cs.at[8 + s], cr.at[8 + s])
    low[0].wait_recv()
    low[2].start()
    for s in range(4):
        pd = ((rx + nr - 2 * s) % nr, cy)
        arrived(pd, (yr if s % 2 else xr).at[4 + s // 2])
        send(pd, k_dev, cs.at[12 + s], cr.at[12 + s])
    cky = (ck + 2) % 4
    for t, (i, j) in enumerate(((r, ck), (rx, ck), (r, cky), (rx, cky))):
        for s in range(4):
            arrived(((i + nr - 2 * s) % nr, j), cr.at[4 * t + s])
    low[1].wait_recv()
    low[2].wait_recv()
    for piece, done in sent:
        each(piece, done)
    for cp in low:
        cp.wait_send()
    for cp in keep:
        cp.wait()


def gather_rows(x):
    tile = x.shape[1:]
    dma = lambda n: pltpu.SemaphoreType.DMA((n,))
    any_ = pl.BlockSpec(memory_space=pl.ANY)
    return pl.pallas_call(
        gather_kernel,
        out_shape=[jax.ShapeDtypeStruct((8, 4, *tile), x.dtype), jax.ShapeDtypeStruct((4, *tile), x.dtype)],
        in_specs=[any_],
        out_specs=[any_, any_],
        scratch_shapes=[dma(3), dma(3), dma(6), dma(6), dma(7), dma(7), dma(18), dma(18), dma(2)],
        compiler_params=pltpu.CompilerParams(collective_id=0, has_side_effects=True),
        name="gather",
    )(x)


def run_panel(p, idx, ntile, nown, sizes, *arrays):
    tc, uc, nc = sizes
    per = PANEL // B
    nrow = ntile - p * per + nown
    width = PANEL + uc * nc + p * 2 * PANEL
    vm = pl.BlockSpec(memory_space=pltpu.VMEM)
    shape = [jax.ShapeDtypeStruct((2, B, tc), jnp.float32)]
    if p == 0:
        shape.append(jax.ShapeDtypeStruct((nrow - per, B, PANEL), jnp.float32))
    return pl.pallas_call(
        functools.partial(panel_kernel, p, ntile, nown, sizes),
        out_shape=shape,
        in_specs=[pl.BlockSpec(memory_space=pltpu.SMEM)] + [vm] * len(arrays),
        out_specs=[vm] * len(shape),
        scratch_shapes=[
            pltpu.VMEM((nrow, B, width), jnp.bfloat16),
            pltpu.VMEM((nrow, B, width), jnp.bfloat16),
            pltpu.VMEM((nrow, B, PANEL), jnp.float32),
            pltpu.VMEM((nrow, B, B), jnp.bfloat16),
            pltpu.VMEM((nrow, B, B), jnp.bfloat16),
            pltpu.VMEM((B, B), jnp.float32),
            pltpu.VMEM((H, 2 * H), jnp.float32),
        ],
        cost_estimate=pl.CostEstimate(flops=60_000_000_000, bytes_accessed=30_000_000, transcendentals=0),
        compiler_params=pltpu.CompilerParams(vmem_limit_bytes=60 * 2**20),
        name="panel%d" % p,
    )(idx, *arrays)


def per_device(factor, update):
    blocks, tile_rows, panels, tc = factor.shape
    uc = update.shape[2]
    nr, nc = lax.axis_size("row"), lax.axis_size("col")
    r, c = lax.axis_index("row"), lax.axis_index("col")
    ntile = PANELS * PANEL // tile_rows
    if (nr, nc, blocks, panels, tile_rows, tc, uc) == (NTOP, 4, 2, 2, B, B, H):
        x = factor.reshape(2, B, 4, H).transpose(0, 2, 1, 3)
        x = jnp.concatenate([update[:, None], x], axis=1)
        idx = jnp.stack([r, c]).astype(jnp.int32)
        return run_top(idx, *gather_rows(x)).transpose(0, 2, 1, 3)
    whole_rows = nr == ntile
    nown = blocks - 1 if whole_rows else blocks
    sizes = (tc, uc, nc)
    xa = jnp.concatenate([factor[:, :, 0], update], axis=2)
    xb = factor[:, :, 1]

    def diag(x):
        if whole_rows:
            return lax.all_gather(x, ("row", "col")).reshape(ntile, nc, *x.shape)
        tiles = [lax.psum(jnp.where(r == t, x, 0.0), "row") for t in range(ntile)]
        return jnp.moveaxis(lax.all_gather(jnp.stack(tiles), "col"), 0, 1)

    def own(x):
        return jnp.moveaxis(lax.all_gather(x[blocks - nown :], "col"), 0, 1)

    da, oa = diag(xa[0]), own(xa)
    xb = xb + (da[0, 0, 0, 0] + oa[0, 0, 0, 0]) * 0.0
    db, ob = diag(xb[0]), own(xb)
    idx = jnp.stack([r, c]).astype(jnp.int32)
    out0, f0 = run_panel(0, idx, ntile, nown, sizes, da, oa)
    (out1,) = run_panel(1, idx, ntile, nown, sizes, da[ntile // 2 :], oa, db[ntile // 2 :], ob, f0)
    out = jnp.stack([out0, out1], axis=2)
    if not whole_rows:
        rows = (
            jnp.arange(blocks)[:, None] * (nr * tile_rows) + r * tile_rows + jnp.arange(tile_rows)
        )
        cols = jnp.arange(panels)[:, None] * PANEL + c * tc + jnp.arange(tc)
        out = jnp.where(cols <= rows[:, :, None, None], out, 0.0)
    return out


def solution(mesh):
    in_specs = (P(None, "row", None, "col"), P(None, "row", "col"))
    out_specs = P(None, "row", None, "col")
    return jax.shard_map(
        per_device, mesh=mesh, in_specs=in_specs, out_specs=out_specs, check_vma=False
    )
```

```python
import functools

import jax
import jax.numpy as jnp
from jax import lax
from jax.experimental import pallas as pl
from jax.experimental.pallas import tpu as pltpu
from jax.sharding import PartitionSpec as P

PANEL = 1024
PANELS = 2
B=256; H=128; GRP=8; AHEAD=3
NN=(((1,),(0,)),((),()))
NT=(((1,),(1,)),((),())); TN=(((0,),(0,)),((),()))
def split(x):
    hi=x.astype(jnp.bfloat16); return hi,(x-hi.astype(jnp.float32)).astype(jnp.bfloat16)
def dot3(a,b,dims=NT):
    (ah,al),(bh,bl)=a,b
    d=functools.partial(lax.dot_general,dimension_numbers=dims,preferred_element_type=jnp.float32)
    return d(ah,bh)+(d(ah,bl)+d(al,bh))
def small(a,b,dims=NT):
    return dot3(split(a),split(b),dims)
def wide(x):
    return jnp.broadcast_to(x, (GRP, H))


def factor_half(s_ref, a, hook=None):
    rows = lax.broadcasted_iota(jnp.int32, (H, H), 0)
    cols = lax.broadcasted_iota(jnp.int32, (H, H), 1)
    s_ref[:, :H] = a
    s_ref[:, H:] = (rows == cols).astype(jnp.float32)
    sub = lax.broadcasted_iota(jnp.int32, (GRP, 1), 0)
    n = H // GRP
    live = {}
    ahead = None
    for g in range(n):
        j = g * GRP
        near = range(g, min(g + AHEAD + 1, n))
        for h in near:
            if h not in live:
                live[h] = [s_ref[h * GRP : (h + 1) * GRP, :H], s_ref[h * GRP : (h + 1) * GRP, H:]]
        cb = {h: [wide(live[h][0][:, j + b : j + b + 1]) for b in range(GRP)] for h in near if h > g or ahead is None}
        if ahead is not None:
            cb[g] = ahead
        ahead = None
        if g + 1 < n:
            ahead = [wide(live[g + 1][0][:, j + GRP + b : j + GRP + b + 1]) for b in range(GRP)]
        scale = None
        for i in range(GRP):
            if hook is not None:
                hook(g, i)
            piv = [wide(cb[g][b][i : i + 1, :]) for b in range(i, GRP)]
            rs = lax.rsqrt(piv[0])
            inv = rs * rs
            scale = rs if scale is None else jnp.where(sub == i, rs, scale)
            u = [wide(x[i : i + 1, :]) for x in live[g]]
            for h in near:
                p = cb[h][i]
                if h == g:
                    p = jnp.where(sub > i, p, 0.0)
                m = p * inv
                live[h] = [x - m * y for x, y in zip(live[h], u)]
                for b in range(i + 1, GRP):
                    cb[h][b] = cb[h][b] - (p * piv[b - i]) * inv
                if h == g + 1:
                    ahead = [x - m * wide(p[b : b + 1, :]) for b, x in enumerate(ahead)]
        done = [x * scale for x in live.pop(g)]
        s_ref[j : j + GRP, :H], s_ref[j : j + GRP, H:] = done
        lo = (g + AHEAD + 1) * GRP
        if lo < H:
            r = jnp.concatenate(done, axis=1)
            s_ref[lo:, :] = s_ref[lo:, :] - small(r[:, lo:H], r, TN)
    u = jnp.where(rows <= cols, s_ref[:, :H], 0.0)
    return u, s_ref[:, H:]


def factor_panel(nrow, ncol, g, ph, plo, inv, s_ref):
    def step(k, _):
        kc = pl.ds(pl.multiple_of(k * B, B), B)
        a = g[k, :, kc]
        u1, v1 = factor_half(s_ref, a[:H, :H])
        l21 = small(a[H:, :H], v1, NT)
        u2, v2 = factor_half(s_ref, a[H:, H:] - small(l21, l21, NT))
        zero = jnp.zeros((H, H), jnp.float32)
        inv[:H, :H] = v1
        inv[:H, H:] = zero
        inv[H:, :H] = -small(v2, small(l21, v1, NN), NN)
        inv[H:, H:] = v2
        g[k, :H, kc] = jnp.concatenate([u1.T, zero], axis=1)
        g[k, H:, kc] = jnp.concatenate([l21, u2.T], axis=1)
        iv = split(inv[...])

        def panel(i, _):
            p = dot3(split(g[i, :, kc]), iv)
            g[i, :, kc] = p
            ph[i], plo[i] = split(p)
            return 0

        lax.fori_loop(k + 1, nrow, panel, 0)

        def colup(j, _):
            jc = pl.ds(pl.multiple_of(j * B, B), B)
            w = (ph[j], plo[j])

            def rowup(i, _):
                g[i, :, jc] = g[i, :, jc] - dot3((ph[i], plo[i]), w)
                return 0

            lax.fori_loop(j, nrow, rowup, 0)
            return 0

        lax.fori_loop(k + 1, ncol, colup, 0)
        return 0

    lax.fori_loop(0, ncol, step, 0)


def panel_kernel(p, ntile, nown, sizes, *refs):
    tc, uc, ncol_dev = sizes
    per = PANEL // B
    first = p * per
    nrow = ntile - first + nown
    if p == 0:
        idx, d_ref, o_ref, out_ref, f_out, xh, xl, g, ph, plo, inv, s_ref = refs
    else:
        idx, d_ref, o_ref, d1_ref, o1_ref, f_in, out_ref, xh, xl, g, ph, plo, inv, s_ref = refs
    width = PANEL + uc * ncol_dev
    for i in range(nrow):
        t = i + first
        src = d_ref if t < ntile else o_ref
        at = (i if p else t) if t < ntile else t - ntile
        for c in range(ncol_dev):
            xh[i, :, c * tc : (c + 1) * tc], xl[i, :, c * tc : (c + 1) * tc] = split(src[at, c, :, :tc])
            lo = PANEL + c * uc
            xh[i, :, lo : lo + uc], xl[i, :, lo : lo + uc] = split(src[at, c, :, tc:])
        if p:
            src = d1_ref if t < ntile else o1_ref
            for c in range(ncol_dev):
                lo = width + c * tc
                xh[i, :, lo : lo + tc], xl[i, :, lo : lo + tc] = split(src[at, c])
            xh[i, :, width + PANEL :], xl[i, :, width + PANEL :] = split(f_in[i])
    full = width + p * PANEL

    def gram_col(j, _):
        jc = pl.ds(pl.multiple_of(j * B, B), B)

        def gram_row(i, _):
            v = dot3((xh[i, :, :full], xl[i, :, :full]), (xh[j, :, :full], xl[j, :, :full]))
            if p:
                v = v - dot3((xh[i, :, full:], xl[i, :, full:]), (xh[j, :, full:], xl[j, :, full:]))
            g[i, :, jc] = v
            return 0

        lax.fori_loop(j, nrow, gram_row, 0)
        return 0

    lax.fori_loop(0, per, gram_col, 0)
    factor_panel(nrow, per, g, ph, plo, inv, s_ref)
    if p == 0:
        f_out[...] = g[per:]
    oc = pl.ds(pl.multiple_of(idx[1] * tc, tc), tc)
    if nown == 1:
        r = idx[0] - first
        t = g[jnp.maximum(r, 0), :, oc]
        keep = idx[1] * (tc // B) <= r
        out_ref[0] = jnp.where(keep, t, 0.0)
        out_ref[1] = g[nrow - 1, :, oc]
    else:
        for e in range(2):
            out_ref[e] = g[nrow - 2 + e, :, oc]


TASKS = 3
BATCH = 3
NTOP = 8


def tri(i, m):
    return i * (i + 1) // 2 + m


def xtile(i, m):
    return 2 * (NTOP + 1) + tri(i, m)


def ltile(i, m):
    return 2 * (NTOP + 1) + tri(NTOP, NTOP) + i * (i - 1) // 2 + m


NW = tri(NTOP, NTOP) + 1
NPOOL = ltile(NTOP, NTOP) + 1


def plan(slots, late=()):
    jobs = []
    for i in range(NTOP + 1):
        for m in range(min(i, NTOP - 1) + 1):
            due = m if m < i else m - 1
            for q in range(2):
                jobs.append((due, 0, (tri(i, m), 2 * i + q, 2 * m + q, 1)))
            for q in range(m + 1):
                jobs.append((due, 0, (tri(i, m), xtile(i, q), xtile(m, q), 1)))
            for q in range(m if m < i else m - 1):
                jobs.append((due, q + 1, (tri(i, m), ltile(i, q), ltile(m, q), -1)))
    first = [t for due, _, t in jobs if due < 0]
    jobs = sorted((j for j in jobs if j[0] >= 0), key=lambda j: (j[0], -j[1]))
    table = []
    for k in range(NTOP):
        now = [j for j in jobs if j[1] <= k][:slots]
        jobs = [j for j in jobs if j not in now]
        assert not jobs or jobs[0][0] > k
        table += [t for _, _, t in now] + [(NW - 1, 0, 0, 1)] * (slots - len(now))
    return first, table


def split_into(ph, plo, t, x, lanes=slice(None)):
    ph[t, :, lanes], plo[t, :, lanes] = split(x)


def top_kernel(slots, first, pos, tab, g_ref, o_ref, out_ref, ph, plo, w, inv, s_ref, stage, sems):
    n = NTOP
    deep = 3

    def fetch(i):
        m = 3 if i < n // 2 else 5
        src = o_ref if i == n else g_ref.at[i, :, pl.ds(0, m)]
        return pltpu.make_async_copy(src, stage.at[i % deep, :, pl.ds(0, m)], sems.at[i % deep])

    for i in range(deep - 1):
        fetch(i).start()

    def clear(t, _):
        w[t] = jnp.zeros((B, B), jnp.float32)
        return 0

    lax.fori_loop(0, NW, clear, 0)
    for i in range(n + 1):
        if i + deep - 1 <= n:
            fetch(i + deep - 1).start()
        fetch(i).wait()
        for c in range(4):
            lo = (c % 2) * H
            split_into(ph, plo, 2 * i + c // 2, stage[i % deep, c, 0], slice(lo, lo + H))
            for p in range(2):
                m = 4 * p + c
                if m <= i:
                    for h in range(2):
                        split_into(ph, plo, xtile(i, m), stage[i % deep, c, 1 + 2 * p + h], slice(h * H, (h + 1) * H))

    def product(a, b):
        return dot3((ph[a], plo[a]), (ph[b], plo[b]))

    for t, a, b, s in first:
        w[t] = w[t] + s * product(a, b)

    def step(k, _):
        def task(half, g, i):
            for u in range(TASKS):
                if (g % 2) * 8 + i == u * 16 // TASKS:
                    at = k * slots + half * (slots // 2) + (g // 2) * TASKS + u
                    t = tab[at, 0]
                    sign = tab[at, 3].astype(jnp.float32)
                    w[t] = w[t] + sign * product(tab[at, 1], tab[at, 2])

        d = tri(k, k)
        u1, v1 = factor_half(s_ref, w[d, :H, :H], functools.partial(task, 0))
        l21 = small(w[d, H:, :H], v1, NT)
        u2, v2 = factor_half(s_ref, w[d, H:, H:] - small(l21, l21, NT), functools.partial(task, 1))
        zero = jnp.zeros((H, H), jnp.float32)
        inv[:H, :H] = v1
        inv[:H, H:] = zero
        inv[H:, :H] = -small(v2, small(l21, v1, NN), NN)
        inv[H:, H:] = v2
        w[d, :H, :] = jnp.concatenate([u1.T, zero], axis=1)
        w[d, H:, :] = jnp.concatenate([l21, u2.T], axis=1)
        iv = split(inv[...])

        def solve(u, _):
            at, to, x = [], [], []
            for v in range(BATCH):
                i = k + 1 + BATCH * u + v
                spare = (i > n).astype(jnp.int32) if v else 0
                i = i - spare * (i - n)
                at.append(tri(i, k) + spare * (NW - 1 - tri(n, k)) if v else tri(i, k))
                to.append(ltile(i, k) + spare * (NPOOL - 1 - ltile(n, k)) if v else ltile(i, k))
                x.append(split(w[at[v]]))
            x = [dot3(y, iv) for y in x]
            for v in range(BATCH):
                w[at[v]] = x[v]
                split_into(ph, plo, to[v], x[v])
            return 0

        lax.fori_loop(0, (n - k + BATCH - 1) // BATCH, solve, 0)
        t = tri(k + 1, k + 1)
        a = ltile(k + 1, k)
        w[t] = w[t] - product(a, a)
        return 0

    lax.fori_loop(0, n, step, 0)
    r = pos[0]
    for p in range(2):
        m = pos[1] + 4 * p
        out_ref[0, p] = jnp.where(m <= r, w[jnp.where(m <= r, tri(r, m), 0)], 0.0)
        out_ref[1, p] = w[tri(n, m)]


def run_top(pos, gathered, own):
    slots = 2 * (H // GRP) * TASKS // 2
    first, table = plan(slots)
    any_ = pl.BlockSpec(memory_space=pl.ANY)
    smem = pl.BlockSpec(memory_space=pltpu.SMEM)
    return pl.pallas_call(
        functools.partial(top_kernel, slots, first),
        out_shape=jax.ShapeDtypeStruct((2, 2, B, B), jnp.float32),
        in_specs=[smem, smem, any_, any_],
        out_specs=pl.BlockSpec(memory_space=pltpu.VMEM),
        scratch_shapes=[
            pltpu.VMEM((NPOOL, B, B), jnp.bfloat16),
            pltpu.VMEM((NPOOL, B, B), jnp.bfloat16),
            pltpu.VMEM((NW, B, B), jnp.float32),
            pltpu.VMEM((B, B), jnp.float32),
            pltpu.VMEM((H, 2 * H), jnp.float32),
            pltpu.VMEM((3, 4, 5, B, H), jnp.float32),
            pltpu.SemaphoreType.DMA((3,)),
        ],
        cost_estimate=pl.CostEstimate(flops=40_000_000_000, bytes_accessed=25_000_000, transcendentals=0),
        compiler_params=pltpu.CompilerParams(vmem_limit_bytes=58 * 2**20),
        name="top",
    )(pos, jnp.asarray(table, jnp.int32), gathered, own)


def gather_kernel(x_ref, g_ref, o_ref, zs, zr, xs, xr, ys, yr, cs, cr, ls):
    r, c = lax.axis_index("row"), lax.axis_index("col")
    rx = r + 1 - 2 * (r % 2)
    cy = (c + 2) % 4
    ck = c + 1 - 2 * (c % 2)
    nr = 8
    line = [((r + 2 * d) % nr, c) for d in range(1, 4)]
    x_dev, y_dev, k_dev = (rx, c), (r, cy), (r, ck)

    barrier = pltpu.get_barrier_semaphore()
    for dev in line + [x_dev, y_dev, k_dev]:
        pl.semaphore_signal(barrier, inc=1, device_id=dev, device_id_type=pl.DeviceIdType.MESH)
    pl.semaphore_wait(barrier, 6)

    def copy(src, dst, dev, ssem, rsem):
        return pltpu.make_async_remote_copy(
            src_ref=src, dst_ref=dst, send_sem=ssem, recv_sem=rsem, device_id=dev, device_id_type=pl.DeviceIdType.MESH
        )

    def each(piece, act):
        i, j = piece
        for n, cond in ((1, i < j), (3, (i >= j) & (i < 4 + j)), (5, i >= 4 + j)):
            pl.when(cond)(functools.partial(act, n))

    sent = []

    def send(piece, dev, ssem, rsem, mine=False):
        i, j = piece

        def make(n):
            src = x_ref.at[0, pl.ds(0, n)] if mine else g_ref.at[i, j, pl.ds(0, n)]
            return copy(src, g_ref.at[i, j, pl.ds(0, n)], dev, ssem, rsem)

        each(piece, lambda n: make(n).start())
        sent.append((piece, lambda n: make(n).wait_send()))

    def arrived(piece, rsem):
        i, j = piece
        at = lambda n: g_ref.at[i, j, pl.ds(0, n)]
        each(piece, lambda n: copy(at(n), at(n), k_dev, cs.at[0], rsem).wait_recv())

    keep = [
        pltpu.make_async_copy(x_ref.at[0], g_ref.at[r, c], ls.at[0]),
        pltpu.make_async_copy(x_ref.at[1], o_ref.at[c], ls.at[1]),
    ]
    for d in range(3):
        send((r, c), line[d], zs.at[d], zr.at[d], True)
    send((r, c), x_dev, xs.at[0], xr.at[0], True)
    send((r, c), y_dev, ys.at[0], yr.at[0], True)
    send((r, c), k_dev, cs.at[0], cr.at[0], True)
    for cp in keep:
        cp.start()
    low = [
        copy(x_ref.at[1], o_ref.at[c], y_dev, ys.at[6], yr.at[6]),
        copy(x_ref.at[1], o_ref.at[c], k_dev, cs.at[16], cr.at[16]),
        copy(o_ref.at[cy], o_ref.at[cy], k_dev, cs.at[17], cr.at[17]),
    ]
    low[0].start()
    low[1].start()
    for d in range(1, 4):
        p = ((r + nr - 2 * d) % nr, c)
        arrived(p, zr.at[d - 1])
        send(p, x_dev, xs.at[d], xr.at[d])
        send(p, y_dev, ys.at[d], yr.at[d])
        send(p, k_dev, cs.at[d], cr.at[d])
    for s in range(4):
        px = ((rx + nr - 2 * s) % nr, c)
        arrived(px, xr.at[s])
        if s % 2:
            send(px, y_dev, ys.at[4 + s // 2], yr.at[4 + s // 2])
        send(px, k_dev, cs.at[4 + s], cr.at[4 + s])
        py = ((r + nr - 2 * s) % nr, cy)
        arrived(py, yr.at[s])
        if s % 2 == 0:
            send(py, x_dev, xs.at[4 + s // 2], xr.at[4 + s // 2])
        send(py, k_dev, cs.at[8 + s], cr.at[8 + s])
    low[0].wait_recv()
    low[2].start()
    for s in range(4):
        pd = ((rx + nr - 2 * s) % nr, cy)
        arrived(pd, (yr if s % 2 else xr).at[4 + s // 2])
        send(pd, k_dev, cs.at[12 + s], cr.at[12 + s])
    cky = (ck + 2) % 4
    for t, (i, j) in enumerate(((r, ck), (rx, ck), (r, cky), (rx, cky))):
        for s in range(4):
            arrived(((i + nr - 2 * s) % nr, j), cr.at[4 * t + s])
    low[1].wait_recv()
    low[2].wait_recv()
    for piece, done in sent:
        each(piece, done)
    for cp in low:
        cp.wait_send()
    for cp in keep:
        cp.wait()


def gather_rows(x):
    tile = x.shape[1:]
    dma = lambda n: pltpu.SemaphoreType.DMA((n,))
    any_ = pl.BlockSpec(memory_space=pl.ANY)
    return pl.pallas_call(
        gather_kernel,
        out_shape=[jax.ShapeDtypeStruct((8, 4, *tile), x.dtype), jax.ShapeDtypeStruct((4, *tile), x.dtype)],
        in_specs=[any_],
        out_specs=[any_, any_],
        scratch_shapes=[dma(3), dma(3), dma(6), dma(6), dma(7), dma(7), dma(18), dma(18), dma(2)],
        compiler_params=pltpu.CompilerParams(collective_id=0, has_side_effects=True),
        name="gather",
    )(x)


def run_panel(p, idx, ntile, nown, sizes, *arrays):
    tc, uc, nc = sizes
    per = PANEL // B
    nrow = ntile - p * per + nown
    width = PANEL + uc * nc + p * 2 * PANEL
    vm = pl.BlockSpec(memory_space=pltpu.VMEM)
    shape = [jax.ShapeDtypeStruct((2, B, tc), jnp.float32)]
    if p == 0:
        shape.append(jax.ShapeDtypeStruct((nrow - per, B, PANEL), jnp.float32))
    return pl.pallas_call(
        functools.partial(panel_kernel, p, ntile, nown, sizes),
        out_shape=shape,
        in_specs=[pl.BlockSpec(memory_space=pltpu.SMEM)] + [vm] * len(arrays),
        out_specs=[vm] * len(shape),
        scratch_shapes=[
            pltpu.VMEM((nrow, B, width), jnp.bfloat16),
            pltpu.VMEM((nrow, B, width), jnp.bfloat16),
            pltpu.VMEM((nrow, B, PANEL), jnp.float32),
            pltpu.VMEM((nrow, B, B), jnp.bfloat16),
            pltpu.VMEM((nrow, B, B), jnp.bfloat16),
            pltpu.VMEM((B, B), jnp.float32),
            pltpu.VMEM((H, 2 * H), jnp.float32),
        ],
        cost_estimate=pl.CostEstimate(flops=60_000_000_000, bytes_accessed=30_000_000, transcendentals=0),
        compiler_params=pltpu.CompilerParams(vmem_limit_bytes=60 * 2**20),
        name="panel%d" % p,
    )(idx, *arrays)


def per_device(factor, update):
    blocks, tile_rows, panels, tc = factor.shape
    uc = update.shape[2]
    nr, nc = lax.axis_size("row"), lax.axis_size("col")
    r, c = lax.axis_index("row"), lax.axis_index("col")
    ntile = PANELS * PANEL // tile_rows
    if (nr, nc, blocks, panels, tile_rows, tc, uc) == (NTOP, 4, 2, 2, B, B, H):
        x = factor.reshape(2, B, 4, H).transpose(0, 2, 1, 3)
        x = jnp.concatenate([update[:, None], x], axis=1)
        idx = jnp.stack([r, c]).astype(jnp.int32)
        return run_top(idx, *gather_rows(x)).transpose(0, 2, 1, 3)
    whole_rows = nr == ntile
    nown = blocks - 1 if whole_rows else blocks
    sizes = (tc, uc, nc)
    xa = jnp.concatenate([factor[:, :, 0], update], axis=2)
    xb = factor[:, :, 1]

    def diag(x):
        if whole_rows:
            return lax.all_gather(x, ("row", "col")).reshape(ntile, nc, *x.shape)
        tiles = [lax.psum(jnp.where(r == t, x, 0.0), "row") for t in range(ntile)]
        return jnp.moveaxis(lax.all_gather(jnp.stack(tiles), "col"), 0, 1)

    def own(x):
        return jnp.moveaxis(lax.all_gather(x[blocks - nown :], "col"), 0, 1)

    da, oa = diag(xa[0]), own(xa)
    xb = xb + (da[0, 0, 0, 0] + oa[0, 0, 0, 0]) * 0.0
    db, ob = diag(xb[0]), own(xb)
    idx = jnp.stack([r, c]).astype(jnp.int32)
    out0, f0 = run_panel(0, idx, ntile, nown, sizes, da, oa)
    (out1,) = run_panel(1, idx, ntile, nown, sizes, da[ntile // 2 :], oa, db[ntile // 2 :], ob, f0)
    out = jnp.stack([out0, out1], axis=2)
    if not whole_rows:
        rows = (
            jnp.arange(blocks)[:, None] * (nr * tile_rows) + r * tile_rows + jnp.arange(tile_rows)
        )
        cols = jnp.arange(panels)[:, None] * PANEL + c * tc + jnp.arange(tc)
        out = jnp.where(cols <= rows[:, :, None, None], out, 0.0)
    return out


def solution(mesh):
    in_specs = (P(None, "row", None, "col"), P(None, "row", "col"))
    out_specs = P(None, "row", None, "col")
    return jax.shard_map(
        per_device, mesh=mesh, in_specs=in_specs, out_specs=out_specs, check_vma=False
    )
```

```python
import functools

import jax
import jax.numpy as jnp
from jax import lax
from jax.experimental import pallas as pl
from jax.experimental.pallas import tpu as pltpu
from jax.sharding import PartitionSpec as P

PANEL = 1024
PANELS = 2
B=256; H=128; GRP=8; AHEAD=3
NN=(((1,),(0,)),((),()))
NT=(((1,),(1,)),((),())); TN=(((0,),(0,)),((),()))
def split(x):
    hi=x.astype(jnp.bfloat16); return hi,(x-hi.astype(jnp.float32)).astype(jnp.bfloat16)
def dot3(a,b,dims=NT):
    (ah,al),(bh,bl)=a,b
    d=functools.partial(lax.dot_general,dimension_numbers=dims,preferred_element_type=jnp.float32)
    return d(ah,bh)+(d(ah,bl)+d(al,bh))
def small(a,b,dims=NT):
    return dot3(split(a),split(b),dims)
def wide(x):
    return jnp.broadcast_to(x, (GRP, H))


def factor_half(s_ref, a, hook=None):
    rows = lax.broadcasted_iota(jnp.int32, (H, H), 0)
    cols = lax.broadcasted_iota(jnp.int32, (H, H), 1)
    s_ref[:, :H] = a
    s_ref[:, H:] = (rows == cols).astype(jnp.float32)
    sub = lax.broadcasted_iota(jnp.int32, (GRP, 1), 0)
    n = H // GRP
    live = {}
    ahead = None
    for g in range(n):
        j = g * GRP
        near = range(g, min(g + AHEAD + 1, n))
        for h in near:
            if h not in live:
                live[h] = [s_ref[h * GRP : (h + 1) * GRP, :H], s_ref[h * GRP : (h + 1) * GRP, H:]]
        cb = {h: [wide(live[h][0][:, j + b : j + b + 1]) for b in range(GRP)] for h in near if h > g or ahead is None}
        if ahead is not None:
            cb[g] = ahead
        ahead = None
        if g + 1 < n:
            ahead = [wide(live[g + 1][0][:, j + GRP + b : j + GRP + b + 1]) for b in range(GRP)]
        scale = None
        for i in range(GRP):
            if hook is not None:
                hook(g, i)
            piv = [wide(cb[g][b][i : i + 1, :]) for b in range(i, GRP)]
            rs = lax.rsqrt(piv[0])
            inv = rs * rs
            scale = rs if scale is None else jnp.where(sub == i, rs, scale)
            u = [wide(x[i : i + 1, :]) for x in live[g]]
            for h in near:
                p = cb[h][i]
                if h == g:
                    p = jnp.where(sub > i, p, 0.0)
                m = p * inv
                live[h] = [x - m * y for x, y in zip(live[h], u)]
                for b in range(i + 1, GRP):
                    cb[h][b] = cb[h][b] - (p * piv[b - i]) * inv
                if h == g + 1:
                    ahead = [x - m * wide(p[b : b + 1, :]) for b, x in enumerate(ahead)]
        done = [x * scale for x in live.pop(g)]
        s_ref[j : j + GRP, :H], s_ref[j : j + GRP, H:] = done
        lo = (g + AHEAD + 1) * GRP
        if lo < H:
            r = jnp.concatenate(done, axis=1)
            s_ref[lo:, :] = s_ref[lo:, :] - small(r[:, lo:H], r, TN)
    u = jnp.where(rows <= cols, s_ref[:, :H], 0.0)
    return u, s_ref[:, H:]


def factor_panel(nrow, ncol, g, ph, plo, inv, s_ref):
    def step(k, _):
        kc = pl.ds(pl.multiple_of(k * B, B), B)
        a = g[k, :, kc]
        u1, v1 = factor_half(s_ref, a[:H, :H])
        l21 = small(a[H:, :H], v1, NT)
        u2, v2 = factor_half(s_ref, a[H:, H:] - small(l21, l21, NT))
        zero = jnp.zeros((H, H), jnp.float32)
        inv[:H, :H] = v1
        inv[:H, H:] = zero
        inv[H:, :H] = -small(v2, small(l21, v1, NN), NN)
        inv[H:, H:] = v2
        g[k, :H, kc] = jnp.concatenate([u1.T, zero], axis=1)
        g[k, H:, kc] = jnp.concatenate([l21, u2.T], axis=1)
        iv = split(inv[...])

        def panel(i, _):
            p = dot3(split(g[i, :, kc]), iv)
            g[i, :, kc] = p
            ph[i], plo[i] = split(p)
            return 0

        lax.fori_loop(k + 1, nrow, panel, 0)

        def colup(j, _):
            jc = pl.ds(pl.multiple_of(j * B, B), B)
            w = (ph[j], plo[j])

            def rowup(i, _):
                g[i, :, jc] = g[i, :, jc] - dot3((ph[i], plo[i]), w)
                return 0

            lax.fori_loop(j, nrow, rowup, 0)
            return 0

        lax.fori_loop(k + 1, ncol, colup, 0)
        return 0

    lax.fori_loop(0, ncol, step, 0)


def panel_kernel(p, ntile, nown, sizes, *refs):
    tc, uc, ncol_dev = sizes
    per = PANEL // B
    first = p * per
    nrow = ntile - first + nown
    if p == 0:
        idx, d_ref, o_ref, out_ref, f_out, xh, xl, g, ph, plo, inv, s_ref = refs
    else:
        idx, d_ref, o_ref, d1_ref, o1_ref, f_in, out_ref, xh, xl, g, ph, plo, inv, s_ref = refs
    width = PANEL + uc * ncol_dev
    for i in range(nrow):
        t = i + first
        src = d_ref if t < ntile else o_ref
        at = (i if p else t) if t < ntile else t - ntile
        for c in range(ncol_dev):
            xh[i, :, c * tc : (c + 1) * tc], xl[i, :, c * tc : (c + 1) * tc] = split(src[at, c, :, :tc])
            lo = PANEL + c * uc
            xh[i, :, lo : lo + uc], xl[i, :, lo : lo + uc] = split(src[at, c, :, tc:])
        if p:
            src = d1_ref if t < ntile else o1_ref
            for c in range(ncol_dev):
                lo = width + c * tc
                xh[i, :, lo : lo + tc], xl[i, :, lo : lo + tc] = split(src[at, c])
            xh[i, :, width + PANEL :], xl[i, :, width + PANEL :] = split(f_in[i])
    full = width + p * PANEL

    def gram_col(j, _):
        jc = pl.ds(pl.multiple_of(j * B, B), B)

        def gram_row(i, _):
            v = dot3((xh[i, :, :full], xl[i, :, :full]), (xh[j, :, :full], xl[j, :, :full]))
            if p:
                v = v - dot3((xh[i, :, full:], xl[i, :, full:]), (xh[j, :, full:], xl[j, :, full:]))
            g[i, :, jc] = v
            return 0

        lax.fori_loop(j, nrow, gram_row, 0)
        return 0

    lax.fori_loop(0, per, gram_col, 0)
    factor_panel(nrow, per, g, ph, plo, inv, s_ref)
    if p == 0:
        f_out[...] = g[per:]
    oc = pl.ds(pl.multiple_of(idx[1] * tc, tc), tc)
    if nown == 1:
        r = idx[0] - first
        t = g[jnp.maximum(r, 0), :, oc]
        keep = idx[1] * (tc // B) <= r
        out_ref[0] = jnp.where(keep, t, 0.0)
        out_ref[1] = g[nrow - 1, :, oc]
    else:
        for e in range(2):
            out_ref[e] = g[nrow - 2 + e, :, oc]


TASKS = 3
BATCH = 3
NTOP = 8


def tri(i, m):
    return i * (i + 1) // 2 + m


def xtile(i, m):
    return 2 * (NTOP + 1) + tri(i, m)


def ltile(i, m):
    return 2 * (NTOP + 1) + tri(NTOP, NTOP) + i * (i - 1) // 2 + m


NW = tri(NTOP, NTOP) + 1
NPOOL = ltile(NTOP, NTOP) + 1


def plan(slots, late=()):
    jobs = []
    for i in range(NTOP + 1):
        for m in range(min(i, NTOP - 1) + 1):
            due = m if m < i else m - 1
            for q in range(2):
                jobs.append((due, 0, (tri(i, m), 2 * i + q, 2 * m + q, 1)))
            for q in range(m + 1):
                jobs.append((due, 0, (tri(i, m), xtile(i, q), xtile(m, q), 1)))
            for q in range(m if m < i else m - 1):
                jobs.append((due, q + 1, (tri(i, m), ltile(i, q), ltile(m, q), -1)))
    first = [t for due, _, t in jobs if due < 0]
    jobs = sorted((j for j in jobs if j[0] >= 0), key=lambda j: (j[0], -j[1]))
    table = []
    for k in range(NTOP):
        now = [j for j in jobs if j[1] <= k][:slots]
        jobs = [j for j in jobs if j not in now]
        assert not jobs or jobs[0][0] > k
        table += [t for _, _, t in now] + [(NW - 1, 0, 0, 1)] * (slots - len(now))
    return first, table


def split_into(ph, plo, t, x, lanes=slice(None)):
    ph[t, :, lanes], plo[t, :, lanes] = split(x)


def top_kernel(slots, first, pos, tab, g_ref, o_ref, out_ref, ph, plo, w, inv, s_ref, stage, sems):
    n = NTOP
    deep = 3

    def fetch(i):
        m = 3 if i < n // 2 else 5
        src = o_ref if i == n else g_ref.at[i, :, pl.ds(0, m)]
        return pltpu.make_async_copy(src, stage.at[i % deep, :, pl.ds(0, m)], sems.at[i % deep])

    for i in range(deep - 1):
        fetch(i).start()

    def clear(t, _):
        w[t] = jnp.zeros((B, B), jnp.float32)
        return 0

    lax.fori_loop(0, NW, clear, 0)
    for i in range(n + 1):
        if i + deep - 1 <= n:
            fetch(i + deep - 1).start()
        fetch(i).wait()
        for c in range(4):
            lo = (c % 2) * H
            split_into(ph, plo, 2 * i + c // 2, stage[i % deep, c, 0], slice(lo, lo + H))
            for p in range(2):
                m = 4 * p + c
                if m <= i:
                    for h in range(2):
                        split_into(ph, plo, xtile(i, m), stage[i % deep, c, 1 + 2 * p + h], slice(h * H, (h + 1) * H))

    def product(a, b):
        return dot3((ph[a], plo[a]), (ph[b], plo[b]))

    for t, a, b, s in first:
        w[t] = w[t] + s * product(a, b)

    def step(k, _):
        def task(half, g, i):
            for u in range(TASKS):
                if (g % 2) * 8 + i == u * 16 // TASKS:
                    at = k * slots + half * (slots // 2) + (g // 2) * TASKS + u
                    t = tab[at, 0]
                    sign = tab[at, 3].astype(jnp.float32)
                    w[t] = w[t] + sign * product(tab[at, 1], tab[at, 2])

        d = tri(k, k)
        u1, v1 = factor_half(s_ref, w[d, :H, :H], functools.partial(task, 0))
        l21 = small(w[d, H:, :H], v1, NT)
        u2, v2 = factor_half(s_ref, w[d, H:, H:] - small(l21, l21, NT), functools.partial(task, 1))
        zero = jnp.zeros((H, H), jnp.float32)
        inv[:H, :H] = v1
        inv[:H, H:] = zero
        inv[H:, :H] = -small(v2, small(l21, v1, NN), NN)
        inv[H:, H:] = v2
        w[d, :H, :H] = u1
        w[d, H:, :] = jnp.concatenate([l21, u2], axis=1)
        iv = split(inv[...])

        def solve(u, _):
            at, to, x = [], [], []
            for v in range(BATCH):
                i = k + 1 + BATCH * u + v
                spare = (i > n).astype(jnp.int32) if v else 0
                i = i - spare * (i - n)
                at.append(tri(i, k) + spare * (NW - 1 - tri(n, k)) if v else tri(i, k))
                to.append(ltile(i, k) + spare * (NPOOL - 1 - ltile(n, k)) if v else ltile(i, k))
                x.append(split(w[at[v]]))
            x = [dot3(y, iv) for y in x]
            for v in range(BATCH):
                w[at[v]] = x[v]
                split_into(ph, plo, to[v], x[v])
            return 0

        lax.fori_loop(0, (n - k + BATCH - 1) // BATCH, solve, 0)
        t = tri(k + 1, k + 1)
        a = ltile(k + 1, k)
        w[t] = w[t] - product(a, a)
        return 0

    lax.fori_loop(0, n, step, 0)
    r = pos[0]
    zero = jnp.zeros((H, H), jnp.float32)
    for p in range(2):
        m = pos[1] + 4 * p
        x = jnp.where(m <= r, w[jnp.where(m <= r, tri(r, m), 0)], 0.0)
        turned = jnp.concatenate(
            [jnp.concatenate([x[:H, :H].T, zero], axis=1), jnp.concatenate([x[H:, :H], x[H:, H:].T], axis=1)], axis=0
        )
        for e, y in enumerate((jnp.where(m == r, turned, x), w[tri(n, m)])):
            for h in range(2):
                out_ref[pl.ds(4 * B * e + 2 * h + p, B, stride=4), :] = y[:, h * H : (h + 1) * H]


def run_top(pos, gathered, own):
    slots = 2 * (H // GRP) * TASKS // 2
    first, table = plan(slots)
    any_ = pl.BlockSpec(memory_space=pl.ANY)
    smem = pl.BlockSpec(memory_space=pltpu.SMEM)
    return pl.pallas_call(
        functools.partial(top_kernel, slots, first),
        out_shape=jax.ShapeDtypeStruct((8 * B, H), jnp.float32),
        in_specs=[smem, smem, any_, any_],
        out_specs=pl.BlockSpec(memory_space=pltpu.VMEM),
        scratch_shapes=[
            pltpu.VMEM((NPOOL, B, B), jnp.bfloat16),
            pltpu.VMEM((NPOOL, B, B), jnp.bfloat16),
            pltpu.VMEM((NW, B, B), jnp.float32),
            pltpu.VMEM((B, B), jnp.float32),
            pltpu.VMEM((H, 2 * H), jnp.float32),
            pltpu.VMEM((3, 4, 5, B, H), jnp.float32),
            pltpu.SemaphoreType.DMA((3,)),
        ],
        cost_estimate=pl.CostEstimate(flops=40_000_000_000, bytes_accessed=25_000_000, transcendentals=0),
        compiler_params=pltpu.CompilerParams(vmem_limit_bytes=58 * 2**20),
        name="top",
    )(pos, jnp.asarray(table, jnp.int32), gathered, own)


def gather_kernel(x_ref, g_ref, o_ref, zs, zr, xs, xr, ys, yr, cs, cr, ls):
    r, c = lax.axis_index("row"), lax.axis_index("col")
    rx = r + 1 - 2 * (r % 2)
    cy = (c + 2) % 4
    ck = c + 1 - 2 * (c % 2)
    nr = 8
    line = [((r + 2 * d) % nr, c) for d in range(1, 4)]
    x_dev, y_dev, k_dev = (rx, c), (r, cy), (r, ck)

    barrier = pltpu.get_barrier_semaphore()
    for dev in line + [x_dev, y_dev, k_dev]:
        pl.semaphore_signal(barrier, inc=1, device_id=dev, device_id_type=pl.DeviceIdType.MESH)
    pl.semaphore_wait(barrier, 6)

    def copy(src, dst, dev, ssem, rsem):
        return pltpu.make_async_remote_copy(
            src_ref=src, dst_ref=dst, send_sem=ssem, recv_sem=rsem, device_id=dev, device_id_type=pl.DeviceIdType.MESH
        )

    def each(piece, act):
        i, j = piece
        for n, cond in ((1, i < j), (3, (i >= j) & (i < 4 + j)), (5, i >= 4 + j)):
            pl.when(cond)(functools.partial(act, n))

    sent = []

    def send(piece, dev, ssem, rsem, mine=False):
        i, j = piece

        def make(n):
            src = x_ref.at[0, pl.ds(0, n)] if mine else g_ref.at[i, j, pl.ds(0, n)]
            return copy(src, g_ref.at[i, j, pl.ds(0, n)], dev, ssem, rsem)

        each(piece, lambda n: make(n).start())
        sent.append((piece, lambda n: make(n).wait_send()))

    def arrived(piece, rsem):
        i, j = piece
        at = lambda n: g_ref.at[i, j, pl.ds(0, n)]
        each(piece, lambda n: copy(at(n), at(n), k_dev, cs.at[0], rsem).wait_recv())

    keep = [
        pltpu.make_async_copy(x_ref.at[0], g_ref.at[r, c], ls.at[0]),
        pltpu.make_async_copy(x_ref.at[1], o_ref.at[c], ls.at[1]),
    ]
    for d in range(3):
        send((r, c), line[d], zs.at[d], zr.at[d], True)
    send((r, c), x_dev, xs.at[0], xr.at[0], True)
    send((r, c), y_dev, ys.at[0], yr.at[0], True)
    send((r, c), k_dev, cs.at[0], cr.at[0], True)
    for cp in keep:
        cp.start()
    low = [
        copy(x_ref.at[1], o_ref.at[c], y_dev, ys.at[6], yr.at[6]),
        copy(x_ref.at[1], o_ref.at[c], k_dev, cs.at[16], cr.at[16]),
        copy(o_ref.at[cy], o_ref.at[cy], k_dev, cs.at[17], cr.at[17]),
    ]
    low[0].start()
    low[1].start()
    for d in range(1, 4):
        p = ((r + nr - 2 * d) % nr, c)
        arrived(p, zr.at[d - 1])
        send(p, x_dev, xs.at[d], xr.at[d])
        send(p, y_dev, ys.at[d], yr.at[d])
        send(p, k_dev, cs.at[d], cr.at[d])
    for s in range(4):
        px = ((rx + nr - 2 * s) % nr, c)
        arrived(px, xr.at[s])
        if s % 2:
            send(px, y_dev, ys.at[4 + s // 2], yr.at[4 + s // 2])
        send(px, k_dev, cs.at[4 + s], cr.at[4 + s])
        py = ((r + nr - 2 * s) % nr, cy)
        arrived(py, yr.at[s])
        if s % 2 == 0:
            send(py, x_dev, xs.at[4 + s // 2], xr.at[4 + s // 2])
        send(py, k_dev, cs.at[8 + s], cr.at[8 + s])
    low[0].wait_recv()
    low[2].start()
    for s in range(4):
        pd = ((rx + nr - 2 * s) % nr, cy)
        arrived(pd, (yr if s % 2 else xr).at[4 + s // 2])
        send(pd, k_dev, cs.at[12 + s], cr.at[12 + s])
    cky = (ck + 2) % 4
    for t, (i, j) in enumerate(((r, ck), (rx, ck), (r, cky), (rx, cky))):
        for s in range(4):
            arrived(((i + nr - 2 * s) % nr, j), cr.at[4 * t + s])
    low[1].wait_recv()
    low[2].wait_recv()
    for piece, done in sent:
        each(piece, done)
    for cp in low:
        cp.wait_send()
    for cp in keep:
        cp.wait()


def gather_rows(x):
    tile = x.shape[1:]
    dma = lambda n: pltpu.SemaphoreType.DMA((n,))
    any_ = pl.BlockSpec(memory_space=pl.ANY)
    return pl.pallas_call(
        gather_kernel,
        out_shape=[jax.ShapeDtypeStruct((8, 4, *tile), x.dtype), jax.ShapeDtypeStruct((4, *tile), x.dtype)],
        in_specs=[any_],
        out_specs=[any_, any_],
        scratch_shapes=[dma(3), dma(3), dma(6), dma(6), dma(7), dma(7), dma(18), dma(18), dma(2)],
        compiler_params=pltpu.CompilerParams(collective_id=0, has_side_effects=True),
        name="gather",
    )(x)


def run_panel(p, idx, ntile, nown, sizes, *arrays):
    tc, uc, nc = sizes
    per = PANEL // B
    nrow = ntile - p * per + nown
    width = PANEL + uc * nc + p * 2 * PANEL
    vm = pl.BlockSpec(memory_space=pltpu.VMEM)
    shape = [jax.ShapeDtypeStruct((2, B, tc), jnp.float32)]
    if p == 0:
        shape.append(jax.ShapeDtypeStruct((nrow - per, B, PANEL), jnp.float32))
    return pl.pallas_call(
        functools.partial(panel_kernel, p, ntile, nown, sizes),
        out_shape=shape,
        in_specs=[pl.BlockSpec(memory_space=pltpu.SMEM)] + [vm] * len(arrays),
        out_specs=[vm] * len(shape),
        scratch_shapes=[
            pltpu.VMEM((nrow, B, width), jnp.bfloat16),
            pltpu.VMEM((nrow, B, width), jnp.bfloat16),
            pltpu.VMEM((nrow, B, PANEL), jnp.float32),
            pltpu.VMEM((nrow, B, B), jnp.bfloat16),
            pltpu.VMEM((nrow, B, B), jnp.bfloat16),
            pltpu.VMEM((B, B), jnp.float32),
            pltpu.VMEM((H, 2 * H), jnp.float32),
        ],
        cost_estimate=pl.CostEstimate(flops=60_000_000_000, bytes_accessed=30_000_000, transcendentals=0),
        compiler_params=pltpu.CompilerParams(vmem_limit_bytes=60 * 2**20),
        name="panel%d" % p,
    )(idx, *arrays)


def per_device(factor, update):
    blocks, tile_rows, panels, tc = factor.shape
    uc = update.shape[2]
    nr, nc = lax.axis_size("row"), lax.axis_size("col")
    r, c = lax.axis_index("row"), lax.axis_index("col")
    ntile = PANELS * PANEL // tile_rows
    if (nr, nc, blocks, panels, tile_rows, tc, uc) == (NTOP, 4, 2, 2, B, B, H):
        x = factor.reshape(2, B, 4, H).transpose(0, 2, 1, 3)
        x = jnp.concatenate([update[:, None], x], axis=1)
        idx = jnp.stack([r, c]).astype(jnp.int32)
        out = run_top(idx, *gather_rows(x)).reshape(2, B, 2, 2, H)
        return out.transpose(0, 1, 3, 2, 4).reshape(2, B, 2, 2 * H)
    whole_rows = nr == ntile
    nown = blocks - 1 if whole_rows else blocks
    sizes = (tc, uc, nc)
    xa = jnp.concatenate([factor[:, :, 0], update], axis=2)
    xb = factor[:, :, 1]

    def diag(x):
        if whole_rows:
            return lax.all_gather(x, ("row", "col")).reshape(ntile, nc, *x.shape)
        tiles = [lax.psum(jnp.where(r == t, x, 0.0), "row") for t in range(ntile)]
        return jnp.moveaxis(lax.all_gather(jnp.stack(tiles), "col"), 0, 1)

    def own(x):
        return jnp.moveaxis(lax.all_gather(x[blocks - nown :], "col"), 0, 1)

    da, oa = diag(xa[0]), own(xa)
    xb = xb + (da[0, 0, 0, 0] + oa[0, 0, 0, 0]) * 0.0
    db, ob = diag(xb[0]), own(xb)
    idx = jnp.stack([r, c]).astype(jnp.int32)
    out0, f0 = run_panel(0, idx, ntile, nown, sizes, da, oa)
    (out1,) = run_panel(1, idx, ntile, nown, sizes, da[ntile // 2 :], oa, db[ntile // 2 :], ob, f0)
    out = jnp.stack([out0, out1], axis=2)
    if not whole_rows:
        rows = (
            jnp.arange(blocks)[:, None] * (nr * tile_rows) + r * tile_rows + jnp.arange(tile_rows)
        )
        cols = jnp.arange(panels)[:, None] * PANEL + c * tc + jnp.arange(tc)
        out = jnp.where(cols <= rows[:, :, None, None], out, 0.0)
    return out


def solution(mesh):
    in_specs = (P(None, "row", None, "col"), P(None, "row", "col"))
    out_specs = P(None, "row", None, "col")
    return jax.shard_map(
        per_device, mesh=mesh, in_specs=in_specs, out_specs=out_specs, check_vma=False
    )
```
